32 devices in a mesh: st: 4 (over y, x), tp: 8 (over z, core).
Axes of the slice: x: 2, y: 2, z: 4, core: 2. Of those that a mesh axis runs over, the one named last changes fastest.
Arguments:
- continuous: bfloat16 [64, 3, 1424], P(('st', 'tp')), may hold values from -48 to 48
- templates: bfloat16 [64, 12, 3, 400], P(('st', 'tp')), may hold values from -120 to 120
- station_list: int32 [64, 12], P(('st', 'tp')), may hold values from 0 to 63, as said below
- moveouts: int32 [64, 12], P(('st', 'tp')), may hold values from 0 to 256
Outputs:
- detection: float32 [64, 768], P(('st', 'tp'))
The draws below stay inside these ranges and needn't reach their ends.
Inputs may be any that keep to these rules, and one draw needn't show every extreme that they name: `station_list`: A station's group is station // 16. The 12 stations of a template are distinct, and so are their indices within their groups (station % 16). The rows of one device (2 templates, aligned blocks in order) name at most 12 stations of any one group, and in every such block one group is named exactly 12 times; blocks b and b2 with b % 8 == b2 % 8 share that group.
All inputs are finite; a program needn't handle non-finite values.
Results may differ from the reference program's by a relative error of at most 0.0003.
Values may be sent and summed in bfloat16 or wider, within the bound.
A program may use at most 64 MiB of HBM per device.

```python
import math
import jax
import jax.numpy as jnp
from jax import lax

TPL_DEV = 2
WIN = 768
TLEN = 400
SHIFT_MAX = 256
CH = 3
NLIST = 12
GROUPS = 4
TGROUPS = 8
STA_GRP = 16
STATIONS = 64
TEMPLATES = 64
CAP = 12
OUT = 1024
DLEN = 1424


def rough_envelope(key, leading, length, block_size, lower, upper):
    block_total = (length + block_size - 1) // block_size
    levels = jnp.exp(jax.random.uniform(key, leading + (block_total,), jnp.float32, math.log(lower), math.log(upper)))
    return jnp.repeat(levels, block_size, axis=-1, total_repeat_length=block_total * block_size)[..., :length]


def draw_continuous(key, part):
    key_wave, key_scale, key_env = jax.random.split(key, 3)
    shape = (STATIONS, CH, DLEN)
    wave = jnp.clip(jax.random.normal(key_wave, shape, jnp.float32), -4.0, 4.0)
    scale = jnp.exp(jax.random.uniform(key_scale, (STATIONS, CH, 1), jnp.float32, math.log(0.2), math.log(4.0)))
    envelope = rough_envelope(key_env, (STATIONS, CH), DLEN, 64, 1.0 / 3.0, 3.0)
    return (wave * scale * envelope).astype(jnp.bfloat16)


def draw_templates(key, part):
    key_wave, key_scale, key_env = jax.random.split(key, 3)
    shape = (TEMPLATES, NLIST, CH, TLEN)
    wave = jnp.clip(jax.random.normal(key_wave, shape, jnp.float32), -4.0, 4.0)
    scale = jnp.exp(jax.random.uniform(key_scale, (TEMPLATES, NLIST, CH, 1), jnp.float32, math.log(0.1), math.log(10.0)))
    envelope = rough_envelope(key_env, (TEMPLATES, NLIST, CH), TLEN, 40, 1.0 / 3.0, 3.0)
    return (wave * scale * envelope).astype(jnp.bfloat16)


def draw_station_list(key, part):
    key_hot, key_groups, key_local = jax.random.split(key, 3)
    block_total = GROUPS * TGROUPS
    entries = NLIST * TPL_DEV
    remaining = entries - CAP
    pool_size = (GROUPS - 1) * CAP
    hot_column = jax.random.randint(key_hot, (TGROUPS,), 0, GROUPS).astype(jnp.int32)
    hot_groups = jnp.tile(hot_column, GROUPS)

    def one_block(block_key, hot_group):
        key_pool, key_order = jax.random.split(block_key)
        others = jnp.arange(pool_size, dtype=jnp.int32) // CAP
        others = others + (others >= hot_group).astype(jnp.int32)
        chosen = jax.random.permutation(key_pool, others)[:remaining]
        listed = jnp.concatenate([jnp.full((CAP,), hot_group, jnp.int32), chosen])
        return jax.random.permutation(key_order, listed)
    groups = jax.vmap(one_block)(jax.random.split(key_groups, block_total), hot_groups).reshape(TEMPLATES, NLIST)

    def pick_local(template_key):
        return jax.random.permutation(template_key, STA_GRP)[:NLIST].astype(jnp.int32)
    local_index = jax.vmap(pick_local)(jax.random.split(key_local, TEMPLATES))
    return (groups * STA_GRP + local_index).astype(jnp.int32)


def place_ends(array, own_key, least, high):
    extent = array.shape
    index_at = [jax.random.randint(jax.random.fold_in(own_key, axis), (), 0, extent[axis]) for axis in range(len(extent))]
    array = array.at[tuple(index_at)].set(least)
    longest = extent.index(max(extent))
    index_at[longest] = (index_at[longest] + 1) % extent[longest]
    return array.at[tuple(index_at)].set(high)


def setup_inputs(seed: int = 0) -> dict:
    seeds = jax.random.split(jax.random.key(seed), 5)
    continuous = draw_continuous(jax.random.fold_in(seeds[4], 71), 0)
    templates = draw_templates(jax.random.fold_in(seeds[4], 71), 0)
    station_list = draw_station_list(jax.random.fold_in(seeds[4], 71), 0)
    moveouts = place_ends(jax.random.randint(seeds[3], (TEMPLATES, NLIST), 0, SHIFT_MAX + 1), jax.random.fold_in(seeds[3], 1), 0, SHIFT_MAX).astype(jnp.int32)
    return dict(continuous=continuous, templates=templates, station_list=station_list, moveouts=moveouts)


EPS = 1e-05

def window_inverse(series):
    squares = jnp.square(series.astype(jnp.float32))
    running = jnp.cumsum(squares, axis=-1)
    running = jnp.concatenate([jnp.zeros(running.shape[:-1] + (1,), jnp.float32), running], axis=-1)
    energy = running[..., TLEN:TLEN + OUT] - running[..., :OUT]
    return lax.rsqrt(energy / TLEN + EPS)

def reference(continuous, templates, station_list, moveouts):
    levels = window_inverse(continuous)
    block_size = math.gcd(TEMPLATES, 8)
    block_total = TEMPLATES // block_size

    def one_block(block_parts):
        block_templates, block_list, block_shift = block_parts
        picked_rows = continuous[block_list]
        scales = levels[block_list]
        channel_total = block_size * NLIST * CH
        signals = picked_rows.reshape(1, channel_total, DLEN).astype(jnp.float32)
        kernels = block_templates.reshape(channel_total, 1, TLEN).astype(jnp.float32)
        products = lax.conv_general_dilated(signals, kernels, (1,), 'VALID', feature_group_count=channel_total, precision=lax.Precision.HIGHEST, dimension_numbers=('NCH', 'OIH', 'NCH'))
        products = products[0, :, :OUT].reshape(block_size, NLIST, CH, OUT)
        template_values = block_templates.astype(jnp.float32)
        template_inverse = lax.rsqrt(lax.optimization_barrier(jnp.mean(template_values * template_values, axis=-1)) + EPS)
        normalized = products * scales * (template_inverse / TLEN)[..., None]
        summed = lax.optimization_barrier(jnp.sum(normalized, axis=2))
        slicer = jax.vmap(jax.vmap(lambda series, start_at: lax.dynamic_slice_in_dim(series, start_at, WIN)))
        aligned = slicer(summed, block_shift)
        return lax.optimization_barrier(jnp.sum(aligned, axis=1))
    grouped = (templates.reshape(block_total, block_size, NLIST, CH, TLEN), station_list.reshape(block_total, block_size, NLIST), moveouts.reshape(block_total, block_size, NLIST))
    result = lax.map(one_block, grouped)
    return result.reshape(TEMPLATES, WIN)
```

```python
import functools

import jax
import jax.numpy as jnp
from jax import lax
from jax.experimental import pallas as pl
from jax.experimental.pallas import tpu as pltpu
from jax.sharding import PartitionSpec as P

WIN = 768
TLEN = 400
CH = 3
DLEN = 1424
EPS = 1e-05
LANES = 128
ROWS = 16
FRAMES = WIN // LANES
STEPS = 5
DEPTH = STEPS * LANES

MESH = pl.DeviceIdType.MESH


def kernel(groups, members, continuous, templates, stations, moveouts, out, records, bands, scales,
           padded, send_sem, recv_sem):
    own = continuous.shape[0]
    template_count, list_size = templates.shape[:2]
    depth_count = members // 2
    st = lax.axis_index("st")
    tp = lax.axis_index("tp")
    z = tp // 2
    core = tp % 2

    def block(group, member):
        return group * members + member

    def rows(index):
        return records.at[pl.ds(index * own, own)]

    def copy(index, send, group, member):
        return pltpu.make_async_remote_copy(
            src_ref=rows(index),
            dst_ref=rows(index),
            send_sem=send_sem.at[send],
            recv_sem=recv_sem.at[index],
            device_id=(group, member),
            device_id_type=MESH,
        )

    def z_peer(step):
        return lax.rem(z + step, depth_count)

    def group_peer(step):
        return lax.rem(st + step, groups)

    partner = z * 2 + 1 - core

    barrier = pltpu.get_barrier_semaphore()
    for step in range(1, depth_count):
        pl.semaphore_signal(barrier, 1, device_id=(st, z_peer(step) * 2 + core), device_id_type=MESH)
    for step in range(1, groups):
        pl.semaphore_signal(barrier, 1, device_id=(group_peer(step), tp), device_id_type=MESH)
    pl.semaphore_signal(barrier, 1, device_id=(st, partner), device_id_type=MESH)

    me = block(st, tp)
    full = DLEN // LANES
    for s in range(own):
        record = continuous[s].astype(jnp.float32)
        for c in range(CH):
            pieces = [record[c : c + 1, n * LANES : (n + 1) * LANES] for n in range(full)]
            tail = jnp.concatenate(
                [record[c : c + 1, full * LANES :],
                 jnp.zeros((1, LANES - (DLEN - full * LANES)), jnp.float32)], axis=1)
            pieces.append(tail)
            pieces.append(jnp.zeros((ROWS - full - 1, LANES), jnp.float32))
            records[me * own + s, c * ROWS : (c + 1) * ROWS, :] = jnp.concatenate(
                pieces, axis=0
            ).astype(jnp.bfloat16)

    pl.semaphore_wait(barrier, depth_count - 1 + groups - 1 + 1)

    xy_base = depth_count - 1
    core_base = xy_base + depth_count * (groups - 1)
    sends = []

    def start(descriptor):
        descriptor.start()
        sends.append(descriptor)

    def to_groups(index, z_step):
        for step in range(1, groups):
            start(copy(index, xy_base + z_step * (groups - 1) + step - 1, group_peer(step), tp))

    def to_partner(index, place):
        start(copy(index, core_base + place, st, partner))

    for step in range(1, depth_count):
        start(copy(me, step - 1, st, z_peer(step) * 2 + core))
    to_groups(me, 0)
    to_partner(me, 0)

    padded[...] = jnp.zeros_like(padded)

    def build(k):
        for t in range(template_count):
            padded[t, k, :, :TLEN] = templates[t, k].astype(jnp.float32)
            wave = padded[t, k]
            energy = jnp.sum(wave * wave, axis=1, keepdims=True)
            scale = lax.rsqrt(energy / TLEN + EPS) / TLEN
            scales[t, k] = jnp.broadcast_to(scale, (CH, LANES))
            for c in range(CH):
                spread = jnp.broadcast_to(wave[c : c + 1], (LANES, DEPTH))
                bands[t, k, c] = pltpu.roll(spread, 0, 1, stride=1, stride_axis=0).astype(
                    jnp.bfloat16
                )

    def build_range(first, last):
        def body(k, carry):
            build(k)
            return carry

        lax.fori_loop(first, last, body, 0)

    third = list_size // 3
    build_range(0, third)

    def arrived(index):
        copy(index, 0, st, tp).wait_recv()

    for step in range(1, depth_count):
        source = block(st, lax.rem(z + depth_count - step, depth_count) * 2 + core)
        arrived(source)
        to_groups(source, step)
        to_partner(source, step)
    build_range(third, 2 * third)
    place = depth_count
    for step in range(1, groups):
        group = lax.rem(st + groups - step, groups)
        for z_step in range(depth_count):
            source = block(group, lax.rem(z + depth_count - z_step, depth_count) * 2 + core)
            arrived(source)
            to_partner(source, place)
            place += 1
    build_range(2 * third, list_size)

    row_at = lax.broadcasted_iota(jnp.int32, (LANES, LANES), 0)
    lane_at = lax.broadcasted_iota(jnp.int32, (LANES, LANES), 1)
    rest = TLEN - 3 * LANES
    window = jnp.concatenate(
        [
            (row_at >= lane_at).astype(jnp.float32),
            jnp.ones((LANES, LANES), jnp.float32),
            (row_at < lane_at + rest).astype(jnp.float32),
            (row_at < lane_at + rest - LANES).astype(jnp.float32),
        ],
        axis=1,
    ).astype(jnp.bfloat16)

    for group_step in range(groups):
        for z_step in range(depth_count):
            source = block(lax.rem(st + group_step, groups),
                           lax.rem(z + z_step, depth_count) * 2 + 1 - core)
            arrived(source)

    total_rows = CH * ROWS
    lane = lax.broadcasted_iota(jnp.int32, (total_rows, LANES), 1)

    def up(values, count):
        return pltpu.roll(values, total_rows - count, 0)

    def entry(t, k):
        shift = moveouts[t, k]
        skip = lax.rem(shift, LANES)
        record = records[stations[t, k]].astype(jnp.float32)
        record = pltpu.roll(record, total_rows - lax.div(shift, LANES), 0)
        record = pltpu.roll(record, lax.rem(LANES - skip, LANES), 1)
        record = jnp.where(lane < LANES - skip, record, up(record, 1))
        square = record * record
        high = square.astype(jnp.bfloat16)
        low = (square - high.astype(jnp.float32)).astype(jnp.bfloat16)
        sums = jnp.dot(high, window, preferred_element_type=jnp.float32) + jnp.dot(
            low, window, preferred_element_type=jnp.float32
        )
        part = [sums[:, n * LANES : (n + 1) * LANES] for n in range(4)]
        energy = part[0] + up(part[1], 1) + up(part[1], 2) + up(part[2], 3) + up(part[3], 4)
        level = lax.rsqrt(energy / TLEN + EPS)
        frames = [record] + [up(record, n) for n in range(1, STEPS)]
        total = jnp.zeros((8, LANES), jnp.float32)
        for c in range(CH):
            at = c * ROWS
            left = jnp.concatenate([f[at : at + 8] for f in frames], axis=1).astype(jnp.bfloat16)
            raw = lax.dot_general(
                left, bands[t, k, c], (((1,), (1,)), ((), ())), preferred_element_type=jnp.float32
            )
            total = total + raw * level[at : at + 8] * scales[t, k, c : c + 1, :]
        return total

    def work(k, totals):
        return tuple(totals[t] + entry(t, k) for t in range(template_count))

    totals = lax.fori_loop(
        0, list_size, work,
        tuple(jnp.zeros((8, LANES), jnp.float32) for _ in range(template_count)))
    for t in range(template_count):
        for n in range(FRAMES):
            out[t : t + 1, n * LANES : (n + 1) * LANES] = totals[t][n : n + 1]
    for descriptor in sends:
        descriptor.wait_send()


def shards(groups, members, continuous, templates, station_list, moveouts):
    own = continuous.shape[0]
    template_count, list_size = templates.shape[:2]
    depth_count = members // 2
    send_count = depth_count - 1 + depth_count * (groups - 1) + depth_count * groups
    vmem = pl.BlockSpec(memory_space=pltpu.VMEM)
    smem = pl.BlockSpec(memory_space=pltpu.SMEM)
    entries = template_count * list_size * CH
    return pl.pallas_call(
        functools.partial(kernel, groups, members),
        out_shape=jax.ShapeDtypeStruct((template_count, WIN), jnp.float32),
        in_specs=[vmem, vmem, smem, smem],
        out_specs=vmem,
        scratch_shapes=[
            pltpu.VMEM((groups * members * own, CH * ROWS, LANES), jnp.bfloat16),
            pltpu.VMEM((template_count, list_size, CH, LANES, DEPTH), jnp.bfloat16),
            pltpu.VMEM((template_count, list_size, CH, LANES), jnp.float32),
            pltpu.VMEM((template_count, list_size, CH, DEPTH), jnp.float32),
            pltpu.SemaphoreType.DMA((send_count,)),
            pltpu.SemaphoreType.DMA((groups * members,)),
        ],
        compiler_params=pltpu.CompilerParams(
            collective_id=0, has_side_effects=True, vmem_limit_bytes=40 * 2**20
        ),
        cost_estimate=pl.CostEstimate(
            flops=entries * 2 * 8 * DEPTH * LANES, bytes_accessed=2**20, transcendentals=entries * 2048
        ),
    )(continuous, templates, station_list, moveouts)


def solution(mesh):
    placed = (
        P(("st", "tp"), None, None),
        P(("st", "tp"), None, None, None),
        P(("st", "tp"), None),
        P(("st", "tp"), None),
    )
    return jax.shard_map(
        functools.partial(shards, mesh.shape["st"], mesh.shape["tp"]),
        mesh=mesh, in_specs=placed, out_specs=P(("st", "tp"), None), check_vma=False
    )
```

```python
import functools

import jax
import jax.numpy as jnp
from jax import lax
from jax.experimental import pallas as pl
from jax.experimental.pallas import tpu as pltpu
from jax.sharding import PartitionSpec as P

WIN = 768
TLEN = 400
CH = 3
DLEN = 1424
EPS = 1e-05
LANES = 128
ROWS = 16
FRAMES = WIN // LANES
LAG = 32
PHASES = LANES // LAG
STEPS = 4
DEPTH = STEPS * LANES
AHEAD = 2

MESH = pl.DeviceIdType.MESH


def kernel(groups, members, continuous, templates, stations, moveouts, out, records, bands, scales,
           padded, shifted, window, send_sem, recv_sem):
    own = continuous.shape[1]
    list_size, _, template_count = templates.shape[:3]
    depth_count = members // 2
    st = lax.axis_index("st")
    tp = lax.axis_index("tp")
    z = tp // 2
    core = tp % 2

    def block(group, member):
        return group * members + member

    def rows(index):
        return records.at[pl.ds(index * own, own)]

    def copy(index, send, group, member):
        return pltpu.make_async_remote_copy(
            src_ref=rows(index),
            dst_ref=rows(index),
            send_sem=send_sem.at[send],
            recv_sem=recv_sem.at[index],
            device_id=(group, member),
            device_id_type=MESH,
        )

    def z_peer(step):
        return lax.rem(z + step, depth_count)

    def group_peer(step):
        return lax.rem(st + step, groups)

    partner = z * 2 + 1 - core

    barrier = pltpu.get_barrier_semaphore()
    for step in range(1, depth_count):
        pl.semaphore_signal(barrier, 1, device_id=(st, z_peer(step) * 2 + core), device_id_type=MESH)
    for step in range(1, groups):
        pl.semaphore_signal(barrier, 1, device_id=(group_peer(step), tp), device_id_type=MESH)
    pl.semaphore_signal(barrier, 1, device_id=(st, partner), device_id_type=MESH)

    me = block(st, tp)
    full = DLEN // LANES
    for c in range(CH):
        record = continuous[c].astype(jnp.float32)
        for s in range(own):
            pieces = [record[s : s + 1, n * LANES : (n + 1) * LANES] for n in range(full)]
            tail = jnp.concatenate(
                [record[s : s + 1, full * LANES :],
                 jnp.zeros((1, LANES - (DLEN - full * LANES)), jnp.float32)], axis=1)
            pieces.append(tail)
            pieces.append(jnp.zeros((ROWS - full - 1, LANES), jnp.float32))
            records[me * own + s, c * ROWS : (c + 1) * ROWS, :] = jnp.concatenate(
                pieces, axis=0
            ).astype(jnp.bfloat16)

    pl.semaphore_wait(barrier, depth_count - 1 + groups - 1 + 1)

    xy_base = depth_count - 1
    core_base = xy_base + depth_count * (groups - 1)
    sends = []

    def start(descriptor):
        descriptor.start()
        sends.append(descriptor)

    def to_groups(index, z_step):
        for step in range(1, groups):
            start(copy(index, xy_base + z_step * (groups - 1) + step - 1, group_peer(step), tp))

    def to_partner(index, place):
        start(copy(index, core_base + place, st, partner))

    for step in range(1, depth_count):
        start(copy(me, step - 1, st, z_peer(step) * 2 + core))
    to_groups(me, 0)
    to_partner(me, 0)

    padded[...] = jnp.zeros_like(padded)

    def build(k):
        for c in range(CH):
            padded[k, c, :, :TLEN] = templates[k, c].astype(jnp.float32)
            wave = padded[k, c]
            energy = jnp.sum(wave * wave, axis=1, keepdims=True)
            scale = lax.rsqrt(energy / TLEN + EPS) / TLEN
            scales[k, c] = jnp.broadcast_to(scale, (template_count, LANES))
            for t in range(template_count):
                spread = jnp.broadcast_to(wave[t : t + 1], (LAG, DEPTH))
                bands[k, t, c * LAG : (c + 1) * LAG, :] = pltpu.roll(
                    spread, 0, 1, stride=1, stride_axis=0
                ).astype(jnp.bfloat16)
        for t in range(template_count):
            bands[k, t, CH * LAG :, :] = jnp.zeros((LANES - CH * LAG, DEPTH), jnp.bfloat16)

    def build_range(first, last):
        def body(k, carry):
            build(k)
            return carry

        lax.fori_loop(first, last, body, 0)

    third = list_size // 3
    build_range(0, third)

    def arrived(index):
        copy(index, 0, st, tp).wait_recv()

    for step in range(1, depth_count):
        source = block(st, lax.rem(z + depth_count - step, depth_count) * 2 + core)
        arrived(source)
        to_groups(source, step)
        to_partner(source, step)
    build_range(third, 2 * third)
    place = depth_count
    for step in range(1, groups):
        group = lax.rem(st + groups - step, groups)
        for z_step in range(depth_count):
            source = block(group, lax.rem(z + depth_count - z_step, depth_count) * 2 + core)
            arrived(source)
            to_partner(source, place)
            place += 1
    build_range(2 * third, list_size)

    reach = (STEPS + 1) * LANES
    row_at = lax.broadcasted_iota(jnp.int32, (reach, LANES), 0)
    lane_at = lax.broadcasted_iota(jnp.int32, (reach, LANES), 1)
    inside = jnp.logical_and(row_at >= lane_at, row_at < lane_at + TLEN)
    window[...] = jnp.where(inside, 1.0, 0.0).astype(jnp.bfloat16)

    for group_step in range(groups):
        for z_step in range(depth_count):
            source = block(lax.rem(st + group_step, groups),
                           lax.rem(z + z_step, depth_count) * 2 + 1 - core)
            arrived(source)

    lane = lax.broadcasted_iota(jnp.int32, (8, LANES), 1)

    def shift_into(slot, t, k):
        record = records[stations[t, k]].astype(jnp.float32)
        for phase in range(PHASES):
            skip = lax.rem(moveouts[t, k] + phase * LAG, LANES)
            shifted[slot, phase] = pltpu.roll(record, lax.rem(LANES - skip, LANES), 1)

    def frames(slot, t, k, phase, c, count):
        shift = moveouts[t, k] + phase * LAG
        first = c * ROWS + lax.div(shift, LANES)
        pieces = [shifted[slot, phase, pl.ds(first + n, 8), :] for n in range(count + 1)]
        here = lane < LANES - lax.rem(shift, LANES)
        return [jnp.where(here, pieces[n], pieces[n + 1]) for n in range(count)]

    def entry(slot, t, k):
        left, high, low = [], [], []
        for c in range(CH):
            for phase in range(PHASES):
                parts = frames(slot, t, k, phase, c, STEPS + 1 if phase == 0 else STEPS)
                left.append(jnp.concatenate(parts[:STEPS], axis=1))
                if phase == 0:
                    square = [part * part for part in parts]
                    rounded = [part.astype(jnp.bfloat16).astype(jnp.float32) for part in square]
                    high.append(jnp.concatenate(rounded, axis=1))
                    low.append(
                        jnp.concatenate([v - r for v, r in zip(square, rounded)], axis=1))
        sums = jnp.dot(
            jnp.concatenate(high + low, axis=0).astype(jnp.bfloat16), window[...],
            preferred_element_type=jnp.float32)
        raw = lax.dot_general(
            jnp.concatenate(left, axis=0).astype(jnp.bfloat16), bands[k, t],
            (((1,), (1,)), ((), ())), preferred_element_type=jnp.float32)
        total = jnp.zeros((8, LANES), jnp.float32)
        for c in range(CH):
            energy = sums[c * 8 : (c + 1) * 8] + sums[(CH + c) * 8 : (CH + c + 1) * 8]
            level = lax.rsqrt(energy / TLEN + EPS)
            lags = None
            for phase in range(PHASES):
                at = (c * PHASES + phase) * 8
                piece = raw[at : at + 8]
                if phase != c:
                    piece = pltpu.roll(piece, (phase - c) % PHASES * LAG, 1)
                lags = piece if phase == 0 else jnp.where(lane < phase * LAG, lags, piece)
            total = total + lags * level * scales[k, c, t : t + 1, :]
        return total

    def work(step, totals):
        totals = list(totals)
        batch = [(t, step * AHEAD + ahead) for ahead in range(AHEAD) for t in range(template_count)]
        for slot, (t, k) in enumerate(batch):
            shift_into(slot, t, k)
        for slot, (t, k) in enumerate(batch):
            totals[t] = totals[t] + entry(slot, t, k)
        return tuple(totals)

    totals = lax.fori_loop(
        0, list_size // AHEAD, work,
        tuple(jnp.zeros((8, LANES), jnp.float32) for _ in range(template_count)))
    for t in range(template_count):
        for n in range(FRAMES):
            out[t : t + 1, n * LANES : (n + 1) * LANES] = totals[t][n : n + 1]
    for descriptor in sends:
        descriptor.wait_send()


def shards(groups, members, continuous, templates, station_list, moveouts):
    own = continuous.shape[0]
    template_count, list_size = templates.shape[:2]
    depth_count = members // 2
    send_count = depth_count - 1 + depth_count * (groups - 1) + depth_count * groups
    vmem = pl.BlockSpec(memory_space=pltpu.VMEM)
    smem = pl.BlockSpec(memory_space=pltpu.SMEM)
    entries = template_count * list_size * CH
    return pl.pallas_call(
        functools.partial(kernel, groups, members),
        out_shape=jax.ShapeDtypeStruct((template_count, WIN), jnp.float32),
        in_specs=[vmem, vmem, smem, smem],
        out_specs=vmem,
        scratch_shapes=[
            pltpu.VMEM((groups * members * own, CH * ROWS, LANES), jnp.bfloat16),
            pltpu.VMEM((list_size, template_count, LANES, DEPTH), jnp.bfloat16),
            pltpu.VMEM((list_size, CH, template_count, LANES), jnp.float32),
            pltpu.VMEM((list_size, CH, template_count, DEPTH), jnp.float32),
            pltpu.VMEM((AHEAD * template_count, PHASES, CH * ROWS, LANES), jnp.float32),
            pltpu.VMEM(((STEPS + 1) * LANES, LANES), jnp.bfloat16),
            pltpu.SemaphoreType.DMA((send_count,)),
            pltpu.SemaphoreType.DMA((groups * members,)),
        ],
        compiler_params=pltpu.CompilerParams(
            collective_id=0, has_side_effects=True, vmem_limit_bytes=40 * 2**20
        ),
        cost_estimate=pl.CostEstimate(
            flops=entries * 2 * 8 * DEPTH * LANES, bytes_accessed=2**20, transcendentals=entries * 2048
        ),
    )(continuous.transpose(1, 0, 2), templates.transpose(1, 2, 0, 3), station_list, moveouts)


def solution(mesh):
    placed = (
        P(("st", "tp"), None, None),
        P(("st", "tp"), None, None, None),
        P(("st", "tp"), None),
        P(("st", "tp"), None),
    )
    return jax.shard_map(
        functools.partial(shards, mesh.shape["st"], mesh.shape["tp"]),
        mesh=mesh, in_specs=placed, out_specs=P(("st", "tp"), None), check_vma=False
    )
```

```python
import functools

import jax
import jax.numpy as jnp
from jax import lax
from jax.experimental import pallas as pl
from jax.experimental.pallas import tpu as pltpu
from jax.sharding import PartitionSpec as P

WIN = 768
TLEN = 400
CH = 3
DLEN = 1424
EPS = 1e-05
LANES = 128
ROWS = 16
FRAMES = WIN // LANES
LAG = 32
PHASES = LANES // LAG
STEPS = 4
DEPTH = STEPS * LANES
AHEAD = 4

MESH = pl.DeviceIdType.MESH


def kernel(groups, members, continuous_in, templates_in, stations_in, moveouts_in, out, continuous,
           templates, stations, moveouts, records, bands, scales, padded, shifted, window, load_sem,
           send_sem, recv_sem):
    loads = [
        pltpu.make_async_copy(source, target, load_sem.at[n])
        for n, (source, target) in enumerate(
            [(continuous_in, continuous), (templates_in, templates),
             (stations_in, stations), (moveouts_in, moveouts)])
    ]
    for load in loads:
        load.start()
    own = continuous.shape[1]
    list_size, _, template_count = templates.shape[:3]
    depth_count = members // 2
    st = lax.axis_index("st")
    tp = lax.axis_index("tp")
    z = tp // 2
    core = tp % 2

    def block(group, member):
        return group * members + member

    def rows(index):
        return records.at[pl.ds(index * own, own)]

    def copy(index, send, group, member):
        return pltpu.make_async_remote_copy(
            src_ref=rows(index),
            dst_ref=rows(index),
            send_sem=send_sem.at[send],
            recv_sem=recv_sem.at[index],
            device_id=(group, member),
            device_id_type=MESH,
        )

    def z_peer(step):
        return lax.rem(z + step, depth_count)

    def group_peer(step):
        return lax.rem(st + step, groups)

    partner = z * 2 + 1 - core

    barrier = pltpu.get_barrier_semaphore()
    for step in range(1, depth_count):
        pl.semaphore_signal(barrier, 1, device_id=(st, z_peer(step) * 2 + core), device_id_type=MESH)
    for step in range(1, groups):
        pl.semaphore_signal(barrier, 1, device_id=(group_peer(step), tp), device_id_type=MESH)
    pl.semaphore_signal(barrier, 1, device_id=(st, partner), device_id_type=MESH)

    loads[0].wait()

    me = block(st, tp)
    full = DLEN // LANES
    for c in range(CH):
        record = continuous[c].astype(jnp.float32)
        for s in range(own):
            pieces = [record[s : s + 1, n * LANES : (n + 1) * LANES] for n in range(full)]
            tail = jnp.concatenate(
                [record[s : s + 1, full * LANES :],
                 jnp.zeros((1, LANES - (DLEN - full * LANES)), jnp.float32)], axis=1)
            pieces.append(tail)
            pieces.append(jnp.zeros((ROWS - full - 1, LANES), jnp.float32))
            records[me * own + s, c * ROWS : (c + 1) * ROWS, :] = jnp.concatenate(
                pieces, axis=0
            ).astype(jnp.bfloat16)

    pl.semaphore_wait(barrier, depth_count - 1 + groups - 1 + 1)

    xy_base = depth_count - 1
    core_base = xy_base + depth_count * (groups - 1)
    sends = []

    def start(descriptor):
        descriptor.start()
        sends.append(descriptor)

    def to_groups(index, z_step):
        for step in range(1, groups):
            start(copy(index, xy_base + z_step * (groups - 1) + step - 1, group_peer(step), tp))

    def to_partner(index, place):
        start(copy(index, core_base + place, st, partner))

    for step in range(1, depth_count):
        start(copy(me, step - 1, st, z_peer(step) * 2 + core))
    to_groups(me, 0)
    to_partner(me, 0)

    loads[1].wait()

    padded[...] = jnp.zeros_like(padded)

    def build(k):
        for c in range(CH):
            padded[k, c, :, :TLEN] = templates[k, c].astype(jnp.float32)
            wave = padded[k, c]
            energy = jnp.sum(wave * wave, axis=1, keepdims=True)
            scale = lax.rsqrt(energy / TLEN + EPS) / TLEN
            scales[k, c] = jnp.broadcast_to(scale, (template_count, LANES))
            for t in range(template_count):
                spread = jnp.broadcast_to(wave[t : t + 1], (LAG, DEPTH))
                bands[k, t, c * LAG : (c + 1) * LAG, :] = pltpu.roll(
                    spread, 0, 1, stride=1, stride_axis=0
                ).astype(jnp.bfloat16)
        for t in range(template_count):
            bands[k, t, CH * LAG :, :] = jnp.zeros((LANES - CH * LAG, DEPTH), jnp.bfloat16)

    def build_range(first, last):
        def body(k, carry):
            build(k)
            return carry

        lax.fori_loop(first, last, body, 0)

    third = list_size // 3
    build_range(0, third)

    def arrived(index):
        copy(index, 0, st, tp).wait_recv()

    for step in range(1, depth_count):
        source = block(st, lax.rem(z + depth_count - step, depth_count) * 2 + core)
        arrived(source)
        to_groups(source, step)
        to_partner(source, step)
    build_range(third, 2 * third)
    place = depth_count
    for step in range(1, groups):
        group = lax.rem(st + groups - step, groups)
        for z_step in range(depth_count):
            source = block(group, lax.rem(z + depth_count - z_step, depth_count) * 2 + core)
            arrived(source)
            to_partner(source, place)
            place += 1
    build_range(2 * third, list_size)

    reach = (STEPS + 1) * LANES
    row_at = lax.broadcasted_iota(jnp.int32, (reach, LANES), 0)
    lane_at = lax.broadcasted_iota(jnp.int32, (reach, LANES), 1)
    inside = jnp.logical_and(row_at >= lane_at, row_at < lane_at + TLEN)
    window[...] = jnp.where(inside, 1.0, 0.0).astype(jnp.bfloat16)

    for group_step in range(groups):
        for z_step in range(depth_count):
            source = block(lax.rem(st + group_step, groups),
                           lax.rem(z + z_step, depth_count) * 2 + 1 - core)
            arrived(source)

    loads[2].wait()
    loads[3].wait()
    lane = lax.broadcasted_iota(jnp.int32, (8, LANES), 1)

    def shift_into(slot, t, k):
        record = records[stations[t, k]].astype(jnp.float32)
        for phase in range(PHASES):
            skip = lax.rem(moveouts[t, k] + phase * LAG, LANES)
            shifted[slot, phase] = pltpu.roll(record, lax.rem(LANES - skip, LANES), 1)

    def frames(slot, t, k, phase, c, count):
        shift = moveouts[t, k] + phase * LAG
        first = c * ROWS + lax.div(shift, LANES)
        pieces = [shifted[slot, phase, pl.ds(first + n, 8), :] for n in range(count + 1)]
        here = lane < LANES - lax.rem(shift, LANES)
        return [jnp.where(here, pieces[n], pieces[n + 1]) for n in range(count)]

    def gather(slot, t, k):
        left, high, low = [], [], []
        for c in range(CH):
            for phase in range(PHASES):
                parts = frames(slot, t, k, phase, c, STEPS + 1 if phase == 0 else STEPS)
                left.append(jnp.concatenate(parts[:STEPS], axis=1))
                if phase == 0:
                    square = [part * part for part in parts]
                    rounded = [part.astype(jnp.bfloat16).astype(jnp.float32) for part in square]
                    high.append(jnp.concatenate(rounded, axis=1))
                    low.append(
                        jnp.concatenate([v - r for v, r in zip(square, rounded)], axis=1))
        raw = lax.dot_general(
            jnp.concatenate(left, axis=0).astype(jnp.bfloat16), bands[k, t],
            (((1,), (1,)), ((), ())), preferred_element_type=jnp.float32)
        return raw, jnp.concatenate(high + low, axis=0).astype(jnp.bfloat16)

    def finish(raw, sums, t, k):
        total = jnp.zeros((8, LANES), jnp.float32)
        for c in range(CH):
            energy = sums[c * 8 : (c + 1) * 8] + sums[(CH + c) * 8 : (CH + c + 1) * 8]
            level = lax.rsqrt(energy / TLEN + EPS)
            lags = None
            for phase in range(PHASES):
                at = (c * PHASES + phase) * 8
                piece = raw[at : at + 8]
                if phase != c:
                    piece = pltpu.roll(piece, (phase - c) % PHASES * LAG, 1)
                lags = piece if phase == 0 else jnp.where(lane < phase * LAG, lags, piece)
            total = total + lags * level * scales[k, c, t : t + 1, :]
        return total

    def work(step, totals):
        totals = list(totals)
        batch = [(t, step * AHEAD + ahead) for ahead in range(AHEAD) for t in range(template_count)]
        for slot, (t, k) in enumerate(batch):
            shift_into(slot, t, k)
        gathered = [gather(slot, t, k) for slot, (t, k) in enumerate(batch)]
        sums = jnp.dot(
            jnp.concatenate([squares for _, squares in gathered], axis=0), window[...],
            preferred_element_type=jnp.float32)
        each = 2 * CH * 8
        for slot, (t, k) in enumerate(batch):
            totals[t] = totals[t] + finish(
                gathered[slot][0], sums[slot * each : (slot + 1) * each], t, k)
        return tuple(totals)

    totals = lax.fori_loop(
        0, list_size // AHEAD, work,
        tuple(jnp.zeros((8, LANES), jnp.float32) for _ in range(template_count)))
    for t in range(template_count):
        for n in range(FRAMES):
            out[t : t + 1, n * LANES : (n + 1) * LANES] = totals[t][n : n + 1]
    for descriptor in sends:
        descriptor.wait_send()


def shards(groups, members, continuous, templates, station_list, moveouts):
    own = continuous.shape[0]
    template_count, list_size = templates.shape[:2]
    depth_count = members // 2
    send_count = depth_count - 1 + depth_count * (groups - 1) + depth_count * groups
    waves = continuous.transpose(1, 0, 2)
    shapes = templates.transpose(1, 2, 0, 3)
    entries = template_count * list_size * CH
    return pl.pallas_call(
        functools.partial(kernel, groups, members),
        out_shape=jax.ShapeDtypeStruct((template_count, WIN), jnp.float32),
        in_specs=[pl.BlockSpec(memory_space=pltpu.HBM)] * 4,
        out_specs=pl.BlockSpec(memory_space=pltpu.VMEM),
        scratch_shapes=[
            pltpu.VMEM(waves.shape, waves.dtype),
            pltpu.VMEM(shapes.shape, shapes.dtype),
            pltpu.SMEM(station_list.shape, jnp.int32),
            pltpu.SMEM(moveouts.shape, jnp.int32),
            pltpu.VMEM((groups * members * own, CH * ROWS, LANES), jnp.bfloat16),
            pltpu.VMEM((list_size, template_count, LANES, DEPTH), jnp.bfloat16),
            pltpu.VMEM((list_size, CH, template_count, LANES), jnp.float32),
            pltpu.VMEM((list_size, CH, template_count, DEPTH), jnp.float32),
            pltpu.VMEM((AHEAD * template_count, PHASES, CH * ROWS, LANES), jnp.float32),
            pltpu.VMEM(((STEPS + 1) * LANES, LANES), jnp.bfloat16),
            pltpu.SemaphoreType.DMA((4,)),
            pltpu.SemaphoreType.DMA((send_count,)),
            pltpu.SemaphoreType.DMA((groups * members,)),
        ],
        compiler_params=pltpu.CompilerParams(
            collective_id=0, has_side_effects=True, vmem_limit_bytes=64 * 2**20
        ),
        cost_estimate=pl.CostEstimate(
            flops=entries * 2 * 8 * DEPTH * LANES, bytes_accessed=2**20, transcendentals=entries * 2048
        ),
    )(waves, shapes, station_list, moveouts)


def solution(mesh):
    placed = (
        P(("st", "tp"), None, None),
        P(("st", "tp"), None, None, None),
        P(("st", "tp"), None),
        P(("st", "tp"), None),
    )
    return jax.shard_map(
        functools.partial(shards, mesh.shape["st"], mesh.shape["tp"]),
        mesh=mesh, in_specs=placed, out_specs=P(("st", "tp"), None), check_vma=False
    )
```

```python
import functools

import jax
import jax.numpy as jnp
from jax import lax
from jax.experimental import pallas as pl
from jax.experimental.pallas import tpu as pltpu
from jax.sharding import PartitionSpec as P

WIN = 768
TLEN = 400
CH = 3
DLEN = 1424
EPS = 1e-05
LANES = 128
ROWS = 12
STATION = 40
FRAMES = WIN // LANES
LAG = 32
PHASES = LANES // LAG
STEPS = 4
DEPTH = STEPS * LANES
AHEAD = 4

MESH = pl.DeviceIdType.MESH


def kernel(groups, members, continuous_in, templates_in, stations_in, moveouts_in, out, continuous,
           templates, stations, moveouts, records, bands, scales, padded, shifted, window, load_sem,
           send_sem, recv_sem):
    loads = [
        pltpu.make_async_copy(source, target, load_sem.at[n])
        for n, (source, target) in enumerate(
            [(continuous_in, continuous), (templates_in, templates),
             (stations_in, stations), (moveouts_in, moveouts)])
    ]
    for load in loads:
        load.start()
    own = continuous.shape[1]
    list_size, _, template_count = templates.shape[:3]
    depth_count = members // 2
    st = lax.axis_index("st")
    tp = lax.axis_index("tp")
    z = tp // 2
    core = tp % 2

    def block(group, member):
        return group * members + member

    def rows(index):
        return records.at[index]

    def copy(index, send, group, member):
        return pltpu.make_async_remote_copy(
            src_ref=rows(index),
            dst_ref=rows(index),
            send_sem=send_sem.at[send],
            recv_sem=recv_sem.at[index],
            device_id=(group, member),
            device_id_type=MESH,
        )

    def z_peer(step):
        return lax.rem(z + step, depth_count)

    def group_peer(step):
        return lax.rem(st + step, groups)

    square_group = groups == 4
    if square_group:
        along_x = st + 1 - 2 * lax.rem(st, 2)
        along_y = lax.rem(st + 2, 4)
        first = along_x + core * (along_y - along_x)
        second = along_y + core * (along_x - along_y)
        direct = [second, first]
    else:
        direct = [group_peer(step) for step in range(1, groups)]

    partner = z * 2 + 1 - core

    barrier = pltpu.get_barrier_semaphore()
    for step in range(1, depth_count):
        pl.semaphore_signal(barrier, 1, device_id=(st, z_peer(step) * 2 + core), device_id_type=MESH)
    for group in direct:
        pl.semaphore_signal(barrier, 1, device_id=(group, tp), device_id_type=MESH)
    pl.semaphore_signal(barrier, 1, device_id=(st, partner), device_id_type=MESH)

    loads[0].wait()

    me = block(st, tp)
    full = DLEN // LANES
    pieces = []
    for s in range(own):
        for c in range(CH):
            record = continuous[c].astype(jnp.float32)[s : s + 1]
            pieces += [record[:, n * LANES : (n + 1) * LANES] for n in range(full)]
            pieces.append(jnp.concatenate(
                [record[:, full * LANES :],
                 jnp.zeros((1, LANES - (DLEN - full * LANES)), jnp.float32)], axis=1))
        pieces.append(jnp.zeros((STATION - CH * ROWS, LANES), jnp.float32))
    if records.shape[1] > own * STATION:
        pieces.append(jnp.zeros((records.shape[1] - own * STATION, LANES), jnp.float32))
    records[me] = jnp.concatenate(pieces, axis=0).astype(jnp.bfloat16)

    pl.semaphore_wait(barrier, depth_count - 1 + len(direct) + 1)

    xy_base = depth_count - 1
    core_base = xy_base + depth_count * (groups - 1)
    sends = []

    def start(descriptor):
        descriptor.start()
        sends.append(descriptor)

    def to_groups(index, z_step):
        for place, group in enumerate(direct):
            start(copy(index, xy_base + z_step * (groups - 1) + place, group, tp))

    def forward(index, z_step):
        start(copy(index, xy_base + z_step * (groups - 1) + 2, first, tp))

    def to_partner(index, place):
        start(copy(index, core_base + place, st, partner))

    for step in range(1, depth_count):
        start(copy(me, step - 1, st, z_peer(step) * 2 + core))
    to_groups(me, 0)
    to_partner(me, 0)

    loads[1].wait()

    padded[...] = jnp.zeros_like(padded)

    def build(k):
        waves = []
        for c in range(CH):
            padded[k, c, :, :TLEN] = templates[k, c].astype(jnp.float32)
            wave = padded[k, c]
            energy = jnp.sum(wave * wave, axis=1, keepdims=True)
            scale = lax.rsqrt(energy / TLEN + EPS) / TLEN
            scales[k, c] = jnp.broadcast_to(scale, (template_count, LANES))
            waves.append(wave)
        for t in range(template_count):
            turned = [
                pltpu.roll(
                    jnp.broadcast_to(wave[t : t + 1], (LAG, DEPTH)), 0, 1, stride=1, stride_axis=0
                )
                for wave in waves
            ]
            turned.append(jnp.zeros((LANES - CH * LAG, DEPTH), jnp.float32))
            bands[k, t] = jnp.concatenate(turned, axis=0).T.astype(jnp.bfloat16)

    def build_range(first, last):
        def body(k, carry):
            build(k)
            return carry

        lax.fori_loop(first, last, body, 0)

    def quarter(n):
        build_range(n * list_size // 4, (n + 1) * list_size // 4)

    def arrived(index):
        copy(index, 0, st, tp).wait_recv()

    def from_z(group, step):
        return block(group, lax.rem(z + depth_count - step, depth_count) * 2 + core)

    quarter(0)
    for step in range(1, depth_count):
        source = from_z(st, step)
        arrived(source)
        to_groups(source, step)
        to_partner(source, step)
    quarter(1)
    place = depth_count
    others = [second, first, 3 - st] if square_group else [
        lax.rem(st + groups - step, groups) for step in range(1, groups)]
    for number, group in enumerate(others):
        for step in range(depth_count):
            source = from_z(group, step)
            arrived(source)
            if square_group and number == 0:
                forward(source, step)
            to_partner(source, place)
            place += 1
        if number == 0:
            quarter(2)
    quarter(3)

    reach = (STEPS + 1) * LANES
    row_at = lax.broadcasted_iota(jnp.int32, (reach, LANES), 0)
    lane_at = lax.broadcasted_iota(jnp.int32, (reach, LANES), 1)
    inside = jnp.logical_and(row_at >= lane_at, row_at < lane_at + TLEN)
    window[...] = jnp.where(inside, 1.0, 0.0).astype(jnp.bfloat16)

    for group_step in range(groups):
        for z_step in range(depth_count):
            source = block(lax.rem(st + group_step, groups),
                           lax.rem(z + z_step, depth_count) * 2 + 1 - core)
            arrived(source)

    loads[2].wait()
    loads[3].wait()
    lane = lax.broadcasted_iota(jnp.int32, (8, LANES), 1)

    def shift_into(slot, t, k):
        station = stations[t, k]
        held = records[lax.div(station, own)].astype(jnp.float32)
        record = held[:STATION]
        for s in range(1, own):
            record = jnp.where(
                lax.rem(station, own) == s, held[s * STATION : (s + 1) * STATION], record)
        for phase in range(PHASES):
            skip = lax.rem(moveouts[t, k] + phase * LAG, LANES)
            shifted[slot, phase] = pltpu.roll(record, lax.rem(LANES - skip, LANES), 1)

    def frames(slot, t, k, phase, c, count):
        shift = moveouts[t, k] + phase * LAG
        first = c * ROWS + lax.div(shift, LANES)
        pieces = [shifted[slot, phase, pl.ds(first + n, 8), :] for n in range(count + 1)]
        here = lane < LANES - lax.rem(shift, LANES)
        return [jnp.where(here, pieces[n], pieces[n + 1]) for n in range(count)]

    def gather(slot, t, k):
        left, high, low = [], [], []
        for c in range(CH):
            for phase in range(PHASES):
                parts = frames(slot, t, k, phase, c, STEPS + 1 if phase == 0 else STEPS)
                left.append(jnp.concatenate(parts[:STEPS], axis=1))
                if phase == 0:
                    square = [part * part for part in parts]
                    rounded = [part.astype(jnp.bfloat16).astype(jnp.float32) for part in square]
                    high.append(jnp.concatenate(rounded, axis=1))
                    low.append(
                        jnp.concatenate([v - r for v, r in zip(square, rounded)], axis=1))
        raw = lax.dot_general(
            jnp.concatenate(left, axis=0).astype(jnp.bfloat16), bands[k, t],
            (((1,), (0,)), ((), ())), preferred_element_type=jnp.float32)
        return raw, jnp.concatenate(high + low, axis=0).astype(jnp.bfloat16)

    def finish(raw, sums, t, k):
        total = jnp.zeros((8, LANES), jnp.float32)
        for c in range(CH):
            energy = sums[c * 8 : (c + 1) * 8] + sums[(CH + c) * 8 : (CH + c + 1) * 8]
            level = lax.rsqrt(energy / TLEN + EPS)
            lags = None
            for phase in range(PHASES):
                at = (c * PHASES + phase) * 8
                piece = raw[at : at + 8]
                if phase != c:
                    piece = pltpu.roll(piece, (phase - c) % PHASES * LAG, 1)
                lags = piece if phase == 0 else jnp.where(lane < phase * LAG, lags, piece)
            total = total + lags * level * scales[k, c, t : t + 1, :]
        return total

    def work(step, totals):
        totals = list(totals)
        batch = [(t, step * AHEAD + ahead) for ahead in range(AHEAD) for t in range(template_count)]
        for slot, (t, k) in enumerate(batch):
            shift_into(slot, t, k)
        gathered = [gather(slot, t, k) for slot, (t, k) in enumerate(batch)]
        sums = jnp.dot(
            jnp.concatenate([squares for _, squares in gathered], axis=0), window[...],
            preferred_element_type=jnp.float32)
        each = 2 * CH * 8
        for slot, (t, k) in enumerate(batch):
            totals[t] = totals[t] + finish(
                gathered[slot][0], sums[slot * each : (slot + 1) * each], t, k)
        return tuple(totals)

    totals = lax.fori_loop(
        0, list_size // AHEAD, work,
        tuple(jnp.zeros((8, LANES), jnp.float32) for _ in range(template_count)))
    for t in range(template_count):
        for n in range(FRAMES):
            out[t : t + 1, n * LANES : (n + 1) * LANES] = totals[t][n : n + 1]
    for descriptor in sends:
        descriptor.wait_send()


def shards(groups, members, continuous, templates, station_list, moveouts):
    own = continuous.shape[0]
    template_count, list_size = templates.shape[:2]
    depth_count = members // 2
    send_count = depth_count - 1 + depth_count * (groups - 1) + depth_count * groups
    waves = continuous.transpose(1, 0, 2)
    shapes = templates.transpose(1, 2, 0, 3)
    entries = template_count * list_size * CH
    return pl.pallas_call(
        functools.partial(kernel, groups, members),
        out_shape=jax.ShapeDtypeStruct((template_count, WIN), jnp.float32),
        in_specs=[pl.BlockSpec(memory_space=pltpu.HBM)] * 4,
        out_specs=pl.BlockSpec(memory_space=pltpu.VMEM),
        scratch_shapes=[
            pltpu.VMEM(waves.shape, waves.dtype),
            pltpu.VMEM(shapes.shape, shapes.dtype),
            pltpu.SMEM(station_list.shape, jnp.int32),
            pltpu.SMEM(moveouts.shape, jnp.int32),
            pltpu.VMEM((groups * members, -(-own * STATION // 16) * 16, LANES), jnp.bfloat16),
            pltpu.VMEM((list_size, template_count, DEPTH, LANES), jnp.bfloat16),
            pltpu.VMEM((list_size, CH, template_count, LANES), jnp.float32),
            pltpu.VMEM((list_size, CH, template_count, DEPTH), jnp.float32),
            pltpu.VMEM((AHEAD * template_count, PHASES, STATION, LANES), jnp.float32),
            pltpu.VMEM(((STEPS + 1) * LANES, LANES), jnp.bfloat16),
            pltpu.SemaphoreType.DMA((4,)),
            pltpu.SemaphoreType.DMA((send_count,)),
            pltpu.SemaphoreType.DMA((groups * members,)),
        ],
        compiler_params=pltpu.CompilerParams(
            collective_id=0, has_side_effects=True, vmem_limit_bytes=64 * 2**20
        ),
        cost_estimate=pl.CostEstimate(
            flops=entries * 2 * 8 * DEPTH * LANES, bytes_accessed=2**20, transcendentals=entries * 2048
        ),
    )(waves, shapes, station_list, moveouts)


def solution(mesh):
    placed = (
        P(("st", "tp"), None, None),
        P(("st", "tp"), None, None, None),
        P(("st", "tp"), None),
        P(("st", "tp"), None),
    )
    return jax.shard_map(
        functools.partial(shards, mesh.shape["st"], mesh.shape["tp"]),
        mesh=mesh, in_specs=placed, out_specs=P(("st", "tp"), None), check_vma=False
    )
```

```python
import functools

import jax
import jax.numpy as jnp
from jax import lax
from jax.experimental import pallas as pl
from jax.experimental.pallas import tpu as pltpu
from jax.sharding import PartitionSpec as P

WIN = 768
TLEN = 400
CH = 3
DLEN = 1424
EPS = 1e-05
LANES = 128
ROWS = 12
STATION = 40
FRAMES = WIN // LANES
LAG = 32
PHASES = LANES // LAG
STEPS = 4
DEPTH = STEPS * LANES
AHEAD = 6

MESH = pl.DeviceIdType.MESH


def kernel(groups, members, continuous_in, templates_in, stations_in, moveouts_in, out, continuous,
           templates, stations, moveouts, records, bands, scales, padded, shifted, window, load_sem,
           send_sem, recv_sem):
    loads = [
        pltpu.make_async_copy(source, target, load_sem.at[n])
        for n, (source, target) in enumerate(
            [(continuous_in, continuous), (templates_in, templates),
             (stations_in, stations), (moveouts_in, moveouts)])
    ]
    for load in loads:
        load.start()
    own = continuous.shape[1]
    list_size, _, template_count = templates.shape[:3]
    depth_count = members // 2
    st = lax.axis_index("st")
    tp = lax.axis_index("tp")
    z = tp // 2
    core = tp % 2

    def block(group, member):
        return group * members + member

    def rows(index):
        return records.at[index]

    def copy(index, send, group, member):
        return pltpu.make_async_remote_copy(
            src_ref=rows(index),
            dst_ref=rows(index),
            send_sem=send_sem.at[send],
            recv_sem=recv_sem.at[index],
            device_id=(group, member),
            device_id_type=MESH,
        )

    def z_peer(step):
        return lax.rem(z + step, depth_count)

    def group_peer(step):
        return lax.rem(st + step, groups)

    if groups == 4:
        direct = [st + 1 - 2 * lax.rem(st, 2), lax.rem(st + 2, 4), 3 - st]
    else:
        direct = [group_peer(step) for step in range(1, groups)]
    partner = z * 2 + 1 - core

    barrier = pltpu.get_barrier_semaphore()
    for step in range(1, depth_count):
        pl.semaphore_signal(barrier, 1, device_id=(st, z_peer(step) * 2 + core), device_id_type=MESH)
    for group in direct:
        pl.semaphore_signal(barrier, 1, device_id=(group, tp), device_id_type=MESH)
    pl.semaphore_signal(barrier, 1, device_id=(st, partner), device_id_type=MESH)

    loads[0].wait()

    me = block(st, tp)
    full = DLEN // LANES
    pieces = []
    for s in range(own):
        for c in range(CH):
            record = continuous[c].astype(jnp.float32)[s : s + 1]
            pieces += [record[:, n * LANES : (n + 1) * LANES] for n in range(full)]
            pieces.append(jnp.concatenate(
                [record[:, full * LANES :],
                 jnp.zeros((1, LANES - (DLEN - full * LANES)), jnp.float32)], axis=1))
        pieces.append(jnp.zeros((STATION - CH * ROWS, LANES), jnp.float32))
    if records.shape[1] > own * STATION:
        pieces.append(jnp.zeros((records.shape[1] - own * STATION, LANES), jnp.float32))
    records[me] = jnp.concatenate(pieces, axis=0).astype(jnp.bfloat16)

    pl.semaphore_wait(barrier, depth_count - 1 + len(direct) + 1)

    xy_base = depth_count - 1
    core_base = xy_base + depth_count * (groups - 1)
    sends = []

    def start(descriptor):
        descriptor.start()
        sends.append(descriptor)

    def to_groups(index, z_step):
        for place, group in enumerate(direct):
            start(copy(index, xy_base + z_step * (groups - 1) + place, group, tp))

    def to_partner(index, place):
        start(copy(index, core_base + place, st, partner))

    for step in range(1, depth_count):
        start(copy(me, step - 1, st, z_peer(step) * 2 + core))
    to_groups(me, 0)
    to_partner(me, 0)

    loads[1].wait()

    padded[...] = jnp.zeros_like(padded)

    def build(k):
        waves = []
        for c in range(CH):
            padded[k, c, :, :TLEN] = templates[k, c].astype(jnp.float32)
            wave = padded[k, c]
            energy = jnp.sum(wave * wave, axis=1, keepdims=True)
            scale = lax.rsqrt(energy / TLEN + EPS) / TLEN
            scales[k, c] = jnp.broadcast_to(scale, (template_count, LANES))
            waves.append(wave)
        for t in range(template_count):
            for c, wave in enumerate(waves):
                bands[k, t, c * LAG : (c + 1) * LAG, :] = pltpu.roll(
                    jnp.broadcast_to(wave[t : t + 1], (LAG, DEPTH)), 0, 1, stride=1, stride_axis=0
                ).astype(jnp.bfloat16)
            bands[k, t, CH * LAG :, :] = jnp.zeros((LANES - CH * LAG, DEPTH), jnp.bfloat16)

    def build_range(first, last):
        def body(k, carry):
            build(k)
            return carry

        lax.fori_loop(first, last, body, 0)

    cuts = [0, list_size // 6, list_size // 2, 3 * list_size // 4, list_size]

    def quarter(n):
        build_range(cuts[n], cuts[n + 1])

    def arrived(index):
        copy(index, 0, st, tp).wait_recv()

    def from_z(group, step):
        return block(group, lax.rem(z + depth_count - step, depth_count) * 2 + core)

    quarter(0)
    for step in range(1, depth_count):
        source = from_z(st, step)
        arrived(source)
        to_groups(source, step)
        to_partner(source, step)
    quarter(1)
    place = depth_count
    for number, group in enumerate(direct):
        for step in range(depth_count):
            source = from_z(group, step)
            arrived(source)
            to_partner(source, place)
            place += 1
        if number == 0:
            quarter(2)
    quarter(3)

    reach = (STEPS + 1) * LANES
    row_at = lax.broadcasted_iota(jnp.int32, (reach, LANES), 0)
    lane_at = lax.broadcasted_iota(jnp.int32, (reach, LANES), 1)
    inside = jnp.logical_and(row_at >= lane_at, row_at < lane_at + TLEN)
    window[...] = jnp.where(inside, 1.0, 0.0).astype(jnp.bfloat16)

    for group_step in range(groups):
        for z_step in range(depth_count):
            source = block(lax.rem(st + group_step, groups),
                           lax.rem(z + z_step, depth_count) * 2 + 1 - core)
            arrived(source)

    loads[2].wait()
    loads[3].wait()
    lane = lax.broadcasted_iota(jnp.int32, (8, LANES), 1)

    def shift_into(slot, t, k):
        station = stations[t, k]
        held = records[lax.div(station, own)].astype(jnp.float32)
        record = held[:STATION]
        for s in range(1, own):
            record = jnp.where(
                lax.rem(station, own) == s, held[s * STATION : (s + 1) * STATION], record)
        for phase in range(PHASES):
            skip = lax.rem(moveouts[t, k] + phase * LAG, LANES)
            shifted[slot, phase] = pltpu.roll(record, lax.rem(LANES - skip, LANES), 1)

    def frames(slot, t, k, phase, c, count):
        shift = moveouts[t, k] + phase * LAG
        first = c * ROWS + lax.div(shift, LANES)
        pieces = [shifted[slot, phase, pl.ds(first + n, 8), :] for n in range(count + 1)]
        here = lane < LANES - lax.rem(shift, LANES)
        return [jnp.where(here, pieces[n], pieces[n + 1]) for n in range(count)]

    def gather(slot, t, k):
        left, high, low = [], [], []
        for c in range(CH):
            for phase in range(PHASES):
                parts = frames(slot, t, k, phase, c, STEPS + 1 if phase == 0 else STEPS)
                left.append(jnp.concatenate(parts[:STEPS], axis=1))
                if phase == 0:
                    square = [part * part for part in parts]
                    rounded = [part.astype(jnp.bfloat16).astype(jnp.float32) for part in square]
                    high.append(jnp.concatenate(rounded, axis=1))
                    low.append(
                        jnp.concatenate([v - r for v, r in zip(square, rounded)], axis=1))
        raw = lax.dot_general(
            jnp.concatenate(left, axis=0).astype(jnp.bfloat16), bands[k, t],
            (((1,), (1,)), ((), ())), preferred_element_type=jnp.float32)
        merged = []
        for c in range(CH):
            lags = None
            for phase in range(PHASES):
                at = (c * PHASES + phase) * 8
                piece = raw[at : at + 8]
                if phase != c:
                    piece = pltpu.roll(piece, (phase - c) % PHASES * LAG, 1)
                lags = piece if phase == 0 else jnp.where(lane < phase * LAG, lags, piece)
            merged.append(lags * scales[k, c, t : t + 1, :])
        return merged, jnp.concatenate(high + low, axis=0).astype(jnp.bfloat16)

    def finish(merged, sums):
        total = jnp.zeros((8, LANES), jnp.float32)
        for c in range(CH):
            energy = sums[c * 8 : (c + 1) * 8] + sums[(CH + c) * 8 : (CH + c + 1) * 8]
            total = total + merged[c] * lax.rsqrt(energy / TLEN + EPS)
        return total

    def work(step, totals):
        totals = list(totals)
        batch = [(t, step * AHEAD + ahead) for ahead in range(AHEAD) for t in range(template_count)]
        for slot, (t, k) in enumerate(batch):
            shift_into(slot, t, k)
        gathered = [gather(slot, t, k) for slot, (t, k) in enumerate(batch)]
        sums = jnp.dot(
            jnp.concatenate([squares for _, squares in gathered], axis=0), window[...],
            preferred_element_type=jnp.float32)
        each = 2 * CH * 8
        for slot, (t, k) in enumerate(batch):
            totals[t] = totals[t] + finish(
                gathered[slot][0], sums[slot * each : (slot + 1) * each])
        return tuple(totals)

    totals = lax.fori_loop(
        0, list_size // AHEAD, work,
        tuple(jnp.zeros((8, LANES), jnp.float32) for _ in range(template_count)))
    for t in range(template_count):
        for n in range(FRAMES):
            out[t : t + 1, n * LANES : (n + 1) * LANES] = totals[t][n : n + 1]
    for descriptor in sends:
        descriptor.wait_send()


def shards(groups, members, continuous, templates, station_list, moveouts):
    own = continuous.shape[0]
    template_count, list_size = templates.shape[:2]
    depth_count = members // 2
    send_count = depth_count - 1 + depth_count * (groups - 1) + depth_count * groups
    waves = continuous.transpose(1, 0, 2)
    shapes = templates.transpose(1, 2, 0, 3)
    entries = template_count * list_size * CH
    return pl.pallas_call(
        functools.partial(kernel, groups, members),
        out_shape=jax.ShapeDtypeStruct((template_count, WIN), jnp.float32),
        in_specs=[pl.BlockSpec(memory_space=pltpu.HBM)] * 4,
        out_specs=pl.BlockSpec(memory_space=pltpu.VMEM),
        scratch_shapes=[
            pltpu.VMEM(waves.shape, waves.dtype),
            pltpu.VMEM(shapes.shape, shapes.dtype),
            pltpu.SMEM(station_list.shape, jnp.int32),
            pltpu.SMEM(moveouts.shape, jnp.int32),
            pltpu.VMEM((groups * members, -(-own * STATION // 16) * 16, LANES), jnp.bfloat16),
            pltpu.VMEM((list_size, template_count, LANES, DEPTH), jnp.bfloat16),
            pltpu.VMEM((list_size, CH, template_count, LANES), jnp.float32),
            pltpu.VMEM((list_size, CH, template_count, DEPTH), jnp.float32),
            pltpu.VMEM((AHEAD * template_count, PHASES, STATION, LANES), jnp.float32),
            pltpu.VMEM(((STEPS + 1) * LANES, LANES), jnp.bfloat16),
            pltpu.SemaphoreType.DMA((4,)),
            pltpu.SemaphoreType.DMA((send_count,)),
            pltpu.SemaphoreType.DMA((groups * members,)),
        ],
        compiler_params=pltpu.CompilerParams(
            collective_id=0, has_side_effects=True, vmem_limit_bytes=64 * 2**20
        ),
        cost_estimate=pl.CostEstimate(
            flops=entries * 2 * 8 * DEPTH * LANES, bytes_accessed=2**20, transcendentals=entries * 2048
        ),
    )(waves, shapes, station_list, moveouts)


def solution(mesh):
    placed = (
        P(("st", "tp"), None, None),
        P(("st", "tp"), None, None, None),
        P(("st", "tp"), None),
        P(("st", "tp"), None),
    )
    return jax.shard_map(
        functools.partial(shards, mesh.shape["st"], mesh.shape["tp"]),
        mesh=mesh, in_specs=placed, out_specs=P(("st", "tp"), None), check_vma=False
    )
```

```python
import functools

import jax
import jax.numpy as jnp
from jax import lax
from jax.experimental import pallas as pl
from jax.experimental.pallas import tpu as pltpu
from jax.sharding import PartitionSpec as P

WIN = 768
TLEN = 400
CH = 3
DLEN = 1424
EPS = 1e-05
LANES = 128
ROWS = 12
STATION = 40
FRAMES = WIN // LANES
LAG = 32
PHASES = LANES // LAG
STEPS = 4
DEPTH = STEPS * LANES
AHEAD = 6

MESH = pl.DeviceIdType.MESH


def kernel(groups, members, continuous_in, templates_in, stations_in, moveouts_in, out, continuous,
           templates, stations, moveouts, records, bands, scales, padded, shifted, window, load_sem,
           send_sem, recv_sem):
    loads = [
        pltpu.make_async_copy(source, target, load_sem.at[n])
        for n, (source, target) in enumerate(
            [(continuous_in, continuous), (templates_in, templates),
             (stations_in, stations), (moveouts_in, moveouts)])
    ]
    for load in loads:
        load.start()
    own = continuous.shape[1]
    list_size, _, template_count = templates.shape[:3]
    depth_count = members // 2
    st = lax.axis_index("st")
    tp = lax.axis_index("tp")
    z = tp // 2
    core = tp % 2

    def block(group, member):
        return group * members + member

    def rows(index):
        return records.at[index]

    def copy(index, send, group, member):
        return pltpu.make_async_remote_copy(
            src_ref=rows(index),
            dst_ref=rows(index),
            send_sem=send_sem.at[send],
            recv_sem=recv_sem.at[index],
            device_id=(group, member),
            device_id_type=MESH,
        )

    def z_peer(step):
        return lax.rem(z + step, depth_count)

    def group_peer(step):
        return lax.rem(st + step, groups)

    if groups == 4:
        direct = [st + 1 - 2 * lax.rem(st, 2), lax.rem(st + 2, 4), 3 - st]
    else:
        direct = [group_peer(step) for step in range(1, groups)]
    partner = z * 2 + 1 - core

    barrier = pltpu.get_barrier_semaphore()
    for step in range(1, depth_count):
        pl.semaphore_signal(barrier, 1, device_id=(st, z_peer(step) * 2 + core), device_id_type=MESH)
    for group in direct:
        pl.semaphore_signal(barrier, 1, device_id=(group, tp), device_id_type=MESH)
    pl.semaphore_signal(barrier, 1, device_id=(st, partner), device_id_type=MESH)

    loads[0].wait()

    me = block(st, tp)
    full = DLEN // LANES
    pieces = []
    for s in range(own):
        for c in range(CH):
            record = continuous[c].astype(jnp.float32)[s : s + 1]
            pieces += [record[:, n * LANES : (n + 1) * LANES] for n in range(full)]
            pieces.append(jnp.concatenate(
                [record[:, full * LANES :],
                 jnp.zeros((1, LANES - (DLEN - full * LANES)), jnp.float32)], axis=1))
        pieces.append(jnp.zeros((STATION - CH * ROWS, LANES), jnp.float32))
    if records.shape[1] > own * STATION:
        pieces.append(jnp.zeros((records.shape[1] - own * STATION, LANES), jnp.float32))
    records[me] = jnp.concatenate(pieces, axis=0).astype(jnp.bfloat16)

    pl.semaphore_wait(barrier, depth_count - 1 + len(direct) + 1)

    xy_base = depth_count - 1
    core_base = xy_base + depth_count * (groups - 1)
    sends = []

    def start(descriptor):
        descriptor.start()
        sends.append(descriptor)

    def to_groups(index, z_step):
        for place, group in enumerate(direct):
            start(copy(index, xy_base + z_step * (groups - 1) + place, group, tp))

    def to_partner(index, place):
        start(copy(index, core_base + place, st, partner))

    for step in range(1, depth_count):
        start(copy(me, step - 1, st, z_peer(step) * 2 + core))
    to_groups(me, 0)
    to_partner(me, 0)

    loads[1].wait()

    padded[...] = jnp.zeros_like(padded)

    def build(k):
        waves = []
        for c in range(CH):
            padded[k, c, :, :TLEN] = templates[k, c].astype(jnp.float32)
            wave = padded[k, c]
            energy = jnp.sum(wave * wave, axis=1, keepdims=True)
            scale = lax.rsqrt(energy / TLEN + EPS) / TLEN
            scales[k, c] = jnp.broadcast_to(scale, (template_count, LANES))
            waves.append(wave)
        for t in range(template_count):
            for c, wave in enumerate(waves):
                bands[k, t, c * LAG : (c + 1) * LAG, :] = pltpu.roll(
                    jnp.broadcast_to(wave[t : t + 1], (LAG, DEPTH)), 0, 1, stride=1, stride_axis=0
                ).astype(jnp.bfloat16)
            bands[k, t, CH * LAG :, :] = jnp.zeros((LANES - CH * LAG, DEPTH), jnp.bfloat16)

    def build_range(first, last):
        def body(k, carry):
            build(k)
            return carry

        lax.fori_loop(first, last, body, 0)

    cuts = [0, list_size // 6, list_size // 2, 3 * list_size // 4, list_size]

    def quarter(n):
        build_range(cuts[n], cuts[n + 1])

    def arrived(index):
        copy(index, 0, st, tp).wait_recv()

    def from_z(group, step):
        return block(group, lax.rem(z + depth_count - step, depth_count) * 2 + core)

    quarter(0)
    for step in range(1, depth_count):
        source = from_z(st, step)
        arrived(source)
        to_groups(source, step)
        to_partner(source, step)
    quarter(1)
    place = depth_count
    for number, group in enumerate(direct):
        for step in range(depth_count):
            source = from_z(group, step)
            arrived(source)
            to_partner(source, place)
            place += 1
        if number == 0:
            quarter(2)
    quarter(3)

    reach = (STEPS + 1) * LANES
    row_at = lax.broadcasted_iota(jnp.int32, (reach, LANES), 0)
    lane_at = lax.broadcasted_iota(jnp.int32, (reach, LANES), 1)
    inside = jnp.logical_and(row_at >= lane_at, row_at < lane_at + TLEN)
    window[...] = jnp.where(inside, 1.0, 0.0).astype(jnp.bfloat16)

    for group_step in range(groups):
        for z_step in range(depth_count):
            source = block(lax.rem(st + group_step, groups),
                           lax.rem(z + z_step, depth_count) * 2 + 1 - core)
            arrived(source)

    loads[2].wait()
    loads[3].wait()
    lane = lax.broadcasted_iota(jnp.int32, (8, LANES), 1)

    def shift_into(slot, t, k):
        station = stations[t, k]
        held = records[lax.div(station, own)].astype(jnp.float32)
        record = held[:STATION]
        for s in range(1, own):
            record = jnp.where(
                lax.rem(station, own) == s, held[s * STATION : (s + 1) * STATION], record)
        for phase in range(PHASES):
            skip = lax.rem(moveouts[t, k] + phase * LAG, LANES)
            shifted[slot, phase] = pltpu.roll(record, lax.rem(LANES - skip, LANES), 1)

    def frames(slot, t, k, phase, c, count):
        shift = moveouts[t, k] + phase * LAG
        first = c * ROWS + lax.div(shift, LANES)
        pieces = [shifted[slot, phase, pl.ds(first + n, 8), :] for n in range(count + 1)]
        here = lane < LANES - lax.rem(shift, LANES)
        return [jnp.where(here, pieces[n], pieces[n + 1]) for n in range(count)]

    def gather(slot, t, k):
        left, high, low = [], [], []
        for c in range(CH):
            for phase in range(PHASES):
                parts = frames(slot, t, k, phase, c, STEPS + 1 if phase == 0 else STEPS)
                left.append(jnp.concatenate(parts[:STEPS], axis=1))
                if phase == 0:
                    square = [part * part for part in parts]
                    rounded = [part.astype(jnp.bfloat16).astype(jnp.float32) for part in square]
                    high.append(jnp.concatenate(rounded, axis=1))
                    low.append(
                        jnp.concatenate([v - r for v, r in zip(square, rounded)], axis=1))
        raw = lax.dot_general(
            jnp.concatenate(left, axis=0).astype(jnp.bfloat16), bands[k, t],
            (((1,), (1,)), ((), ())), preferred_element_type=jnp.float32)
        merged = []
        for c in range(CH):
            lags = None
            for phase in range(PHASES):
                at = (c * PHASES + phase) * 8
                piece = raw[at : at + 8]
                if phase != c:
                    piece = pltpu.roll(piece, (phase - c) % PHASES * LAG, 1)
                lags = piece if phase == 0 else jnp.where(lane < phase * LAG, lags, piece)
            merged.append(lags * scales[k, c, t : t + 1, :])
        return merged, jnp.concatenate(high + low, axis=0).astype(jnp.bfloat16)

    def finish(merged, sums):
        total = jnp.zeros((8, LANES), jnp.float32)
        for c in range(CH):
            energy = sums[c * 8 : (c + 1) * 8] + sums[(CH + c) * 8 : (CH + c + 1) * 8]
            total = total + merged[c] * lax.rsqrt(energy / TLEN + EPS)
        return total

    def work(step, totals):
        totals = list(totals)
        batch = [(t, step * AHEAD + ahead) for ahead in range(AHEAD) for t in range(template_count)]
        for slot, (t, k) in enumerate(batch):
            shift_into(slot, t, k)
        gathered = [gather(slot, t, k) for slot, (t, k) in enumerate(batch)]
        sums = jnp.dot(
            jnp.concatenate([squares for _, squares in gathered], axis=0), window[...],
            preferred_element_type=jnp.float32)
        each = 2 * CH * 8
        for slot, (t, k) in enumerate(batch):
            totals[t] = totals[t] + finish(
                gathered[slot][0], sums[slot * each : (slot + 1) * each])
        return tuple(totals)

    totals = lax.fori_loop(
        0, list_size // AHEAD, work,
        tuple(jnp.zeros((8, LANES), jnp.float32) for _ in range(template_count)))
    for t in range(template_count):
        for n in range(FRAMES):
            out[t : t + 1, n * LANES : (n + 1) * LANES] = totals[t][n : n + 1]
    for descriptor in sends:
        descriptor.wait_send()


def shards(groups, members, continuous, templates, station_list, moveouts):
    own = continuous.shape[0]
    template_count, list_size = templates.shape[:2]
    depth_count = members // 2
    send_count = depth_count - 1 + depth_count * (groups - 1) + depth_count * groups
    waves = continuous.transpose(1, 0, 2)
    shapes = templates.transpose(1, 2, 0, 3)
    entries = template_count * list_size * CH
    return pl.pallas_call(
        functools.partial(kernel, groups, members),
        out_shape=pltpu.VMEM((template_count, WIN), jnp.float32),
        in_specs=[pl.BlockSpec(memory_space=pltpu.HBM)] * 4,
        out_specs=pl.BlockSpec(memory_space=pltpu.VMEM),
        scratch_shapes=[
            pltpu.VMEM(waves.shape, waves.dtype),
            pltpu.VMEM(shapes.shape, shapes.dtype),
            pltpu.SMEM(station_list.shape, jnp.int32),
            pltpu.SMEM(moveouts.shape, jnp.int32),
            pltpu.VMEM((groups * members, -(-own * STATION // 16) * 16, LANES), jnp.bfloat16),
            pltpu.VMEM((list_size, template_count, LANES, DEPTH), jnp.bfloat16),
            pltpu.VMEM((list_size, CH, template_count, LANES), jnp.float32),
            pltpu.VMEM((list_size, CH, template_count, DEPTH), jnp.float32),
            pltpu.VMEM((AHEAD * template_count, PHASES, STATION, LANES), jnp.float32),
            pltpu.VMEM(((STEPS + 1) * LANES, LANES), jnp.bfloat16),
            pltpu.SemaphoreType.DMA((4,)),
            pltpu.SemaphoreType.DMA((send_count,)),
            pltpu.SemaphoreType.DMA((groups * members,)),
        ],
        compiler_params=pltpu.CompilerParams(
            collective_id=0, has_side_effects=True, vmem_limit_bytes=48 * 2**20
        ),
        cost_estimate=pl.CostEstimate(
            flops=entries * 2 * 8 * DEPTH * LANES, bytes_accessed=2**20, transcendentals=entries * 2048
        ),
    )(*(pltpu.with_memory_space_constraint(a, pltpu.HBM) for a in (waves, shapes, station_list, moveouts)))


def solution(mesh):
    placed = (
        P(("st", "tp"), None, None),
        P(("st", "tp"), None, None, None),
        P(("st", "tp"), None),
        P(("st", "tp"), None),
    )
    return jax.shard_map(
        functools.partial(shards, mesh.shape["st"], mesh.shape["tp"]),
        mesh=mesh, in_specs=placed, out_specs=P(("st", "tp"), None), check_vma=False
    )
```

```python
import functools

import jax
import jax.numpy as jnp
from jax import lax
from jax.experimental import pallas as pl
from jax.experimental.pallas import tpu as pltpu
from jax.sharding import PartitionSpec as P

WIN = 768
TLEN = 400
CH = 3
DLEN = 1424
EPS = 1e-05
LANES = 128
ROWS = 12
STATION = 40
FRAMES = WIN // LANES
LAG = 32
PHASES = LANES // LAG
STEPS = 4
DEPTH = STEPS * LANES
AHEAD = 6

MESH = pl.DeviceIdType.MESH


def kernel(groups, members, continuous_in, templates_in, stations_in, moveouts_in, out, continuous,
           templates, stations, moveouts, records, bands, scales, padded, shifted, window, load_sem,
           send_sem, recv_sem):
    loads = [
        pltpu.make_async_copy(source, target, load_sem.at[n])
        for n, (source, target) in enumerate(
            [(continuous_in, continuous), (templates_in, templates),
             (stations_in, stations), (moveouts_in, moveouts)])
    ]
    for load in loads:
        load.start()
    own = continuous.shape[1]
    list_size, _, template_count = templates.shape[:3]
    depth_count = members // 2
    st = lax.axis_index("st")
    tp = lax.axis_index("tp")
    z = tp // 2
    core = tp % 2

    def block(group, member):
        return group * members + member

    def rows(index):
        return records.at[index]

    def copy(index, send, group, member):
        return pltpu.make_async_remote_copy(
            src_ref=rows(index),
            dst_ref=rows(index),
            send_sem=send_sem.at[send],
            recv_sem=recv_sem.at[index],
            device_id=(group, member),
            device_id_type=MESH,
        )

    def z_peer(step):
        return lax.rem(z + step, depth_count)

    def group_peer(step):
        return lax.rem(st + step, groups)

    if groups == 4:
        direct = [st + 1 - 2 * lax.rem(st, 2), lax.rem(st + 2, 4), 3 - st]
    else:
        direct = [group_peer(step) for step in range(1, groups)]
    partner = z * 2 + 1 - core

    barrier = pltpu.get_barrier_semaphore()
    for step in range(1, depth_count):
        pl.semaphore_signal(barrier, 1, device_id=(st, z_peer(step) * 2 + core), device_id_type=MESH)
    for group in direct:
        pl.semaphore_signal(barrier, 1, device_id=(group, tp), device_id_type=MESH)
    pl.semaphore_signal(barrier, 1, device_id=(st, partner), device_id_type=MESH)

    reach = (STEPS + 1) * LANES
    row_at = lax.broadcasted_iota(jnp.int32, (reach, LANES), 0)
    lane_at = lax.broadcasted_iota(jnp.int32, (reach, LANES), 1)
    inside = jnp.logical_and(row_at >= lane_at, row_at < lane_at + TLEN)
    window[...] = jnp.where(inside, 1.0, 0.0).astype(jnp.bfloat16)

    padded[...] = jnp.zeros_like(padded)
    bands[:, :, CH * LAG :, :] = jnp.zeros(
        (list_size, template_count, LANES - CH * LAG, DEPTH), jnp.bfloat16)
    loads[0].wait()

    me = block(st, tp)
    full = DLEN // LANES
    pieces = []
    for s in range(own):
        for c in range(CH):
            record = continuous[c].astype(jnp.float32)[s : s + 1]
            pieces += [record[:, n * LANES : (n + 1) * LANES] for n in range(full)]
            pieces.append(jnp.concatenate(
                [record[:, full * LANES :],
                 jnp.zeros((1, LANES - (DLEN - full * LANES)), jnp.float32)], axis=1))
        pieces.append(jnp.zeros((STATION - CH * ROWS, LANES), jnp.float32))
    if records.shape[1] > own * STATION:
        pieces.append(jnp.zeros((records.shape[1] - own * STATION, LANES), jnp.float32))
    records[me] = jnp.concatenate(pieces, axis=0).astype(jnp.bfloat16)

    pl.semaphore_wait(barrier, depth_count - 1 + len(direct) + 1)

    xy_base = depth_count - 1
    core_base = xy_base + depth_count * (groups - 1)
    sends = []

    def start(descriptor):
        descriptor.start()
        sends.append(descriptor)

    def to_groups(index, z_step):
        for place, group in enumerate(direct):
            start(copy(index, xy_base + z_step * (groups - 1) + place, group, tp))

    def to_partner(index, place):
        start(copy(index, core_base + place, st, partner))

    for step in range(1, depth_count):
        start(copy(me, step - 1, st, z_peer(step) * 2 + core))
    to_groups(me, 0)
    to_partner(me, 0)

    loads[1].wait()

    def build(k):
        waves = []
        for c in range(CH):
            padded[k, c, :, :TLEN] = templates[k, c].astype(jnp.float32)
            wave = padded[k, c]
            energy = jnp.sum(wave * wave, axis=1, keepdims=True)
            scale = lax.rsqrt(energy / TLEN + EPS) / TLEN
            scales[k, c] = jnp.broadcast_to(scale, (template_count, LANES))
            waves.append(wave)
        for t in range(template_count):
            for c, wave in enumerate(waves):
                bands[k, t, c * LAG : (c + 1) * LAG, :] = pltpu.roll(
                    jnp.broadcast_to(wave[t : t + 1], (LAG, DEPTH)), 0, 1, stride=1, stride_axis=0
                ).astype(jnp.bfloat16)

    def build_range(first, last):
        def body(k, carry):
            build(k)
            return carry

        lax.fori_loop(first, last, body, 0)

    cuts = [0, list_size // 6, list_size // 2, 3 * list_size // 4, list_size]

    def quarter(n):
        build_range(cuts[n], cuts[n + 1])

    def arrived(index):
        copy(index, 0, st, tp).wait_recv()

    def from_z(group, step):
        return block(group, lax.rem(z + depth_count - step, depth_count) * 2 + core)

    quarter(0)
    for step in range(1, depth_count):
        source = from_z(st, step)
        arrived(source)
        to_groups(source, step)
        to_partner(source, step)
    quarter(1)
    place = depth_count
    for number, group in enumerate(direct):
        for step in range(depth_count):
            source = from_z(group, step)
            arrived(source)
            to_partner(source, place)
            place += 1
        if number == 0:
            quarter(2)
    quarter(3)

    for group_step in range(groups):
        for z_step in range(depth_count):
            source = block(lax.rem(st + group_step, groups),
                           lax.rem(z + z_step, depth_count) * 2 + 1 - core)
            arrived(source)

    loads[2].wait()
    loads[3].wait()
    lane = lax.broadcasted_iota(jnp.int32, (8, LANES), 1)

    def shift_into(slot, t, k):
        station = stations[t, k]
        held = records[lax.div(station, own)].astype(jnp.float32)
        record = held[:STATION]
        for s in range(1, own):
            record = jnp.where(
                lax.rem(station, own) == s, held[s * STATION : (s + 1) * STATION], record)
        for phase in range(PHASES):
            skip = lax.rem(moveouts[t, k] + phase * LAG, LANES)
            shifted[slot, phase] = pltpu.roll(record, lax.rem(LANES - skip, LANES), 1)

    def frames(slot, t, k, phase, c, count):
        shift = moveouts[t, k] + phase * LAG
        first = c * ROWS + lax.div(shift, LANES)
        pieces = [shifted[slot, phase, pl.ds(first + n, 8), :] for n in range(count + 1)]
        here = lane < LANES - lax.rem(shift, LANES)
        return [jnp.where(here, pieces[n], pieces[n + 1]) for n in range(count)]

    def gather(slot, t, k):
        left, high, low = [], [], []
        for c in range(CH):
            for phase in range(PHASES):
                parts = frames(slot, t, k, phase, c, STEPS + 1 if phase == 0 else STEPS)
                left.append(jnp.concatenate(parts[:STEPS], axis=1))
                if phase == 0:
                    square = [part * part for part in parts]
                    rounded = [part.astype(jnp.bfloat16).astype(jnp.float32) for part in square]
                    high.append(jnp.concatenate(rounded, axis=1))
                    low.append(
                        jnp.concatenate([v - r for v, r in zip(square, rounded)], axis=1))
        raw = lax.dot_general(
            jnp.concatenate(left, axis=0).astype(jnp.bfloat16), bands[k, t],
            (((1,), (1,)), ((), ())), preferred_element_type=jnp.float32)
        merged = []
        for c in range(CH):
            lags = None
            for phase in range(PHASES):
                at = (c * PHASES + phase) * 8
                piece = raw[at : at + 8]
                if phase != c:
                    piece = pltpu.roll(piece, (phase - c) % PHASES * LAG, 1)
                lags = piece if phase == 0 else jnp.where(lane < phase * LAG, lags, piece)
            merged.append(lags * scales[k, c, t : t + 1, :])
        return merged, jnp.concatenate(high + low, axis=0).astype(jnp.bfloat16)

    def finish(merged, sums):
        total = jnp.zeros((8, LANES), jnp.float32)
        for c in range(CH):
            energy = sums[c * 8 : (c + 1) * 8] + sums[(CH + c) * 8 : (CH + c + 1) * 8]
            total = total + merged[c] * lax.rsqrt(energy / TLEN + EPS)
        return total

    def work(step, totals):
        totals = list(totals)
        batch = [(t, step * AHEAD + ahead) for ahead in range(AHEAD) for t in range(template_count)]
        for slot, (t, k) in enumerate(batch):
            shift_into(slot, t, k)
        gathered = [gather(slot, t, k) for slot, (t, k) in enumerate(batch)]
        sums = jnp.dot(
            jnp.concatenate([squares for _, squares in gathered], axis=0), window[...],
            preferred_element_type=jnp.float32)
        each = 2 * CH * 8
        for slot, (t, k) in enumerate(batch):
            totals[t] = totals[t] + finish(
                gathered[slot][0], sums[slot * each : (slot + 1) * each])
        return tuple(totals)

    totals = lax.fori_loop(
        0, list_size // AHEAD, work,
        tuple(jnp.zeros((8, LANES), jnp.float32) for _ in range(template_count)))
    for t in range(template_count):
        for n in range(FRAMES):
            out[t : t + 1, n * LANES : (n + 1) * LANES] = totals[t][n : n + 1]
    for descriptor in sends:
        descriptor.wait_send()


def shards(groups, members, continuous, templates, station_list, moveouts):
    own = continuous.shape[0]
    template_count, list_size = templates.shape[:2]
    depth_count = members // 2
    send_count = depth_count - 1 + depth_count * (groups - 1) + depth_count * groups
    waves = continuous.transpose(1, 0, 2)
    shapes = templates.transpose(1, 2, 0, 3)
    entries = template_count * list_size * CH
    return pl.pallas_call(
        functools.partial(kernel, groups, members),
        out_shape=pltpu.VMEM((template_count, WIN), jnp.float32),
        in_specs=[pl.BlockSpec(memory_space=pltpu.HBM)] * 4,
        out_specs=pl.BlockSpec(memory_space=pltpu.VMEM),
        scratch_shapes=[
            pltpu.VMEM(waves.shape, waves.dtype),
            pltpu.VMEM(shapes.shape, shapes.dtype),
            pltpu.SMEM(station_list.shape, jnp.int32),
            pltpu.SMEM(moveouts.shape, jnp.int32),
            pltpu.VMEM((groups * members, -(-own * STATION // 16) * 16, LANES), jnp.bfloat16),
            pltpu.VMEM((list_size, template_count, LANES, DEPTH), jnp.bfloat16),
            pltpu.VMEM((list_size, CH, template_count, LANES), jnp.float32),
            pltpu.VMEM((list_size, CH, template_count, DEPTH), jnp.float32),
            pltpu.VMEM((AHEAD * template_count, PHASES, STATION, LANES), jnp.float32),
            pltpu.VMEM(((STEPS + 1) * LANES, LANES), jnp.bfloat16),
            pltpu.SemaphoreType.DMA((4,)),
            pltpu.SemaphoreType.DMA((send_count,)),
            pltpu.SemaphoreType.DMA((groups * members,)),
        ],
        compiler_params=pltpu.CompilerParams(
            collective_id=0, has_side_effects=True, vmem_limit_bytes=48 * 2**20
        ),
        cost_estimate=pl.CostEstimate(
            flops=entries * 2 * 8 * DEPTH * LANES, bytes_accessed=2**20, transcendentals=entries * 2048
        ),
    )(*(pltpu.with_memory_space_constraint(a, pltpu.HBM) for a in (waves, shapes, station_list, moveouts)))


def solution(mesh):
    placed = (
        P(("st", "tp"), None, None),
        P(("st", "tp"), None, None, None),
        P(("st", "tp"), None),
        P(("st", "tp"), None),
    )
    return jax.shard_map(
        functools.partial(shards, mesh.shape["st"], mesh.shape["tp"]),
        mesh=mesh, in_specs=placed, out_specs=P(("st", "tp"), None), check_vma=False
    )
```
